1024 devices in a mesh: dp: 64 (over z_lo, x, core), sub: 16 (over z_hi, y).
Axes of the slice: x: 4, y: 4, z: 32 (z_hi: 4, z_lo: 8; z = z_hi * 8 + z_lo), core: 2. Of those that a mesh axis runs over, the one named last changes fastest.
Arguments:
- queries: float32 [16384, 4096], P('dp', 'sub'), may hold values from -40 to 40
- passages: float32 [2048, 4096], P(('dp', 'sub')), may hold values from -40 to 40
- positive: int32 [16384], P('dp'), may hold values from 0 to 2047
- hard_negs: int32 [16384, 4], P('dp'), may hold values from 0 to 2047
Outputs:
- row_loss: float32 [16384], P('dp')
- query_grad: float32 [16384, 4096], P('dp', 'sub')
- passage_grad: float32 [2048, 4096], P(('dp', 'sub'))
The draws below stay inside these ranges and needn't reach their ends.
All inputs are finite; a program needn't handle non-finite values.
Results may differ from the reference program's by a relative error of at most 0.015.
Values may be sent and summed in bfloat16 or wider, within the bound.
No kernel may reach another device: no remote copies, remote signals or barrier semaphores. Data moves between devices by JAX's collectives and lax.ppermute only.
A program may use at most 32 MiB of HBM per device.

```python
import math
import jax
import jax.numpy as jnp
from jax import lax

D = 4096
P_DEV = 2
HN = 4
QUERIES = 16384
PASSAGES = 2048
N_DP = 64
N_SUB = 16


def shared_base(key):
    return jax.random.normal(jax.random.fold_in(key, 11), (PASSAGES, D), jnp.float32)


def draw_passages(key, part):
    base = shared_base(key)
    return base


def draw_queries(key, part):
    key = jax.random.fold_in(key, 2)
    own_rows = jax.random.normal(key, (QUERIES, D), jnp.float32)
    return own_rows


def plant(result, key, least, top_value):
    spot = [jax.random.randint(jax.random.fold_in(key, axis), (), 0, length) for axis, length in enumerate(result.shape)]
    longest = result.shape.index(max(result.shape))
    beside = spot[:longest] + [(spot[longest] + 1) % result.shape[longest]] + spot[longest + 1:]
    return result.at[tuple(spot)].set(least).at[tuple(beside)].set(top_value)


def setup_inputs(seed: int = 0) -> dict:
    keys = jax.random.split(jax.random.key(seed), 5)
    return {
        "queries": draw_queries(jax.random.fold_in(keys[4], 71), 0),
        "passages": draw_passages(jax.random.fold_in(keys[4], 71), 0),
        "positive": plant(jax.random.randint(keys[2], (QUERIES,), 0, PASSAGES), jax.random.fold_in(keys[2], 1), 0, PASSAGES - 1).astype(jnp.int32),
        "hard_negs": plant(jax.random.randint(keys[3], (QUERIES, HN), 0, PASSAGES), jax.random.fold_in(keys[3], 1), 0, PASSAGES - 1).astype(jnp.int32),
    }


hard_weight = 4.0

def reference(queries, passages, positive, hard_negs):
    logit_scale = 4.0 / math.sqrt(D)
    qb = queries.astype(jnp.bfloat16)
    pb = passages.astype(jnp.bfloat16)
    column_ids = jnp.arange(PASSAGES, dtype=jnp.int32)
    logits = logit_scale * jnp.dot(qb, pb.T, preferred_element_type=jnp.float32)
    onehot = column_ids[None, :] == positive[:, None].astype(jnp.int32)
    hard_mask = jnp.any(hard_negs[:, :, None].astype(jnp.int32) == column_ids[None, None, :], axis=1)
    hard_mask = jnp.logical_and(hard_mask, jnp.logical_not(onehot))
    weight = jnp.where(hard_mask, jnp.float32(hard_weight), jnp.float32(1.0))
    rowmax = lax.optimization_barrier(jnp.max(logits, axis=1))
    scaled = weight * jnp.exp(logits - rowmax[:, None])
    totals = lax.optimization_barrier(jnp.sum(scaled, axis=1))
    pos_logit = lax.optimization_barrier(jnp.sum(jnp.where(onehot, logits, jnp.float32(0.0)), axis=1))
    row_loss = rowmax + jnp.log(totals) - pos_logit
    dscore = (logit_scale * (scaled / totals[:, None] - onehot.astype(jnp.float32))).astype(jnp.bfloat16)
    passage_grad = jnp.dot(dscore.T, qb, preferred_element_type=jnp.float32)
    share_rows = PASSAGES // N_SUB
    pb_sets = pb.reshape(N_DP, N_SUB, P_DEV, D).transpose(1, 0, 2, 3).reshape(N_SUB, share_rows, D)
    ds_sets = dscore.reshape(QUERIES, N_DP, N_SUB, P_DEV).transpose(2, 0, 1, 3).reshape(N_SUB, QUERIES, share_rows)

    def add_set(carry, pair):
        ds_block, pb_block = pair
        partial_term = jnp.dot(ds_block, pb_block, preferred_element_type=jnp.float32).astype(jnp.bfloat16)
        return (carry + partial_term.astype(jnp.float32), None)
    query_grad, _ = lax.scan(add_set, jnp.zeros((QUERIES, D), jnp.float32), (ds_sets, pb_sets))
    return (row_loss, query_grad, passage_grad)
```

```python
import math

import jax
import jax.numpy as jnp
from jax import lax
from jax.experimental import pallas as pl
from jax.experimental.pallas import tpu as pltpu
from jax.sharding import Mesh, PartitionSpec as P

D = 4096
ZL, X, C, ZH, Y = 8, 4, 2, 4, 4
PLANE = ("x", "c", "y")
XC = ("x", "c")
SUB = ("zh", "y")
G = X * C
hard_weight = 4.0
logit_scale = 4.0 / math.sqrt(D)
bf16, f32 = jnp.bfloat16, jnp.float32
params = pltpu.CompilerParams(vmem_limit_bytes=40 * 2**20)


def exchange(x, axes):
    return lax.all_to_all(x, axes, 0, 0, tiled=True)


def assemble(q_ref, rows_ref):
    groups, parts, n, k = q_ref.shape
    for g in range(groups):
        for s in range(parts):
            rows_ref[g * n : (g + 1) * n, s * k : (s + 1) * k] = q_ref[g, s]


def logits_kernel(q_ref, p_ref, out_ref, rows_ref):
    assemble(q_ref, rows_ref)
    out_ref[...] = lax.dot_general(
        rows_ref[...], p_ref[...], (((1,), (1,)), ((), ())), preferred_element_type=f32
    )


def softmax_kernel(part_ref, ids_ref, ds_ref, loss_ref):
    rows, n = part_ref.shape[1:]
    positive = ids_ref[:, 0:1]
    col = lax.broadcasted_iota(jnp.int32, (rows, n), 1)
    base = (col >> 5) * (G * 32) + (col & 31)
    logits, top = [], None
    for g in range(G):
        a = part_ref[g * Y]
        for y in range(1, Y):
            a = a + part_ref[g * Y + y]
        a = a * logit_scale
        logits.append(a)
        m = jnp.max(a, axis=1, keepdims=True)
        top = m if top is None else jnp.maximum(top, m)
    total = jnp.zeros((rows, 1), f32)
    pos_logit = jnp.zeros((rows, 1), f32)
    scaled, hot = [], []
    for g in range(G):
        ids = base + g * 32
        onehot = ids == positive
        hard = ids == ids_ref[:, 1:2]
        for h in range(2, ids_ref.shape[1]):
            hard = jnp.logical_or(hard, ids == ids_ref[:, h : h + 1])
        hard = jnp.logical_and(hard, jnp.logical_not(onehot))
        e = jnp.where(hard, hard_weight, 1.0) * jnp.exp(logits[g] - top)
        total = total + jnp.sum(e, axis=1, keepdims=True)
        pos_logit = pos_logit + jnp.sum(jnp.where(onehot, logits[g], 0.0), axis=1, keepdims=True)
        scaled.append(e)
        hot.append(jnp.where(onehot, 1.0, 0.0))
    loss_ref[...] = top + jnp.log(total) - pos_logit
    for g in range(G):
        ds = (logit_scale * (scaled[g] / total - hot[g])).astype(bf16)
        for y in range(Y):
            ds_ref[g * Y + y] = ds


def grads_kernel(ds_ref, q_ref, p_ref, qg_ref, pg_ref, rows_ref):
    groups, parts, n, k = q_ref.shape
    assemble(q_ref, rows_ref)
    for g in range(groups):
        terms = jnp.dot(ds_ref[g * n : (g + 1) * n, :], p_ref[...], preferred_element_type=f32)
        for s in range(parts):
            qg_ref[g, s] = terms[:, s * k : (s + 1) * k].astype(bf16)
    pg_ref[...] = lax.dot_general(
        ds_ref[...], rows_ref[...], (((0,), (0,)), ((), ())), preferred_element_type=f32
    ).astype(bf16)


def on_device(queries, passages, positive, hard_negs):
    nq, k = queries.shape
    own = passages.shape[0]
    nz = nq // ZH
    nrow = nz // Y
    width = ZH * k
    sub = lax.axis_index(SUB)

    p = passages.astype(bf16).reshape(own, ZH, Y, k).transpose(2, 0, 1, 3).reshape(Y, own, width)
    p = jnp.broadcast_to(p[None], (ZH, Y, own, width)).reshape(ZH * Y, own, width)
    p = exchange(p, SUB).reshape(ZH * Y * own, width)
    p = jnp.broadcast_to(p[None], (ZL,) + p.shape)
    p = exchange(p, "zl").reshape(ZL * ZH * Y * own, width)

    q = exchange(queries.astype(bf16).reshape(ZH, nz, k), "zh")
    q = exchange(jnp.broadcast_to(q[None], (G,) + q.shape), XC)

    np_ = p.shape[0]
    parts = pl.pallas_call(
        logits_kernel,
        out_shape=jax.ShapeDtypeStruct((G * nz, np_), f32),
        scratch_shapes=[pltpu.VMEM((G * nz, width), bf16)],
        compiler_params=params,
        name="logits",
    )(q, p)
    parts = exchange(parts.reshape(G * Y, nrow, np_), PLANE)

    ids = jnp.concatenate([positive[:, None], hard_negs], axis=1)
    ids = lax.dynamic_slice_in_dim(ids, sub * nrow, nrow, 0)
    ds, loss = pl.pallas_call(
        softmax_kernel,
        out_shape=(
            jax.ShapeDtypeStruct((G * Y, nrow, np_), bf16),
            jax.ShapeDtypeStruct((nrow, 1), f32),
        ),
        compiler_params=params,
        name="softmax",
    )(parts, ids)
    row_loss = exchange(jnp.broadcast_to(loss.reshape(1, nrow), (ZH * Y, nrow)), SUB).reshape(nq)
    ds = exchange(ds, PLANE).reshape(G * nz, np_)

    qg, pg = pl.pallas_call(
        grads_kernel,
        out_shape=(
            jax.ShapeDtypeStruct(q.shape, bf16),
            jax.ShapeDtypeStruct((np_, width), bf16),
        ),
        scratch_shapes=[pltpu.VMEM((G * nz, width), bf16)],
        compiler_params=params,
        name="grads",
    )(ds, q, p)

    pg = exchange(pg.reshape(ZL, np_ // ZL, width), "zl")
    pg = jnp.sum(pg.astype(f32), axis=0).astype(bf16)
    pg = exchange(pg.reshape(ZH * Y, own, width), SUB)
    pg = jnp.sum(pg.astype(f32).reshape(ZH, Y, own, width), axis=0)
    pg = pg.reshape(Y, own, ZH, k).transpose(1, 2, 0, 3).reshape(own, ZH * Y * k)

    qg = jnp.sum(exchange(qg, XC).astype(f32), axis=0).astype(bf16)
    qg = exchange(qg, "zh").reshape(nq, k).astype(f32)
    return row_loss, qg, pg


def solution(mesh):
    fine = Mesh(mesh.devices.reshape(ZL, X, C, ZH, Y), ("zl", "x", "c", "zh", "y"))
    dp, sub = ("zl", "x", "c"), ("zh", "y")
    return jax.shard_map(
        on_device,
        mesh=fine,
        in_specs=(P(dp, sub), P(dp + sub, None), P(dp), P(dp, None)),
        out_specs=(P(dp), P(dp, sub), P(dp + sub, None)),
        check_vma=False,
    )
```

```python
import math

import jax
import jax.numpy as jnp
from jax import lax
from jax.experimental import pallas as pl
from jax.experimental.pallas import tpu as pltpu
from jax.sharding import Mesh, PartitionSpec as P

D = 4096
SIZES = {"za": 2, "zb": 4, "x": 4, "c": 2, "zh": 4, "y": 4}
ZA, ZB, X, C, ZH, Y = SIZES.values()
FAR = ("za", "zh")
NEAR = ("zb", "y")
PLANE = ("x", "c", "y")
G = X * C
A = ZA * ZH
B = ZB * Y
LANES = 128
hard_weight = 4.0
logit_scale = 4.0 / math.sqrt(D)
bf16, f32 = jnp.bfloat16, jnp.float32
params = pltpu.CompilerParams(vmem_limit_bytes=40 * 2**20)
whole = pl.BlockSpec(memory_space=pltpu.VMEM)
scalars = pl.BlockSpec(memory_space=pltpu.SMEM)


def exchange(x, axes):
    return lax.all_to_all(x, axes, 0, 0, tiled=True)


def shift(x, axis, by):
    n = SIZES[axis]
    return lax.ppermute(x, axis, [(i, (i + by) % n) for i in range(n)])


def logits_kernel(at_ref, *refs):
    q_refs, (p_ref, out_ref, rows_ref) = refs[:X], refs[X:]
    n, k = q_refs[0].shape[2:]
    for j in range(X):
        for cc in range(C):
            g = lax.rem(at_ref[0] + X - j, X) * C + lax.rem(at_ref[1] + cc, C)
            for za in range(ZA):
                row = pl.multiple_of(g * (ZA * n) + za * n, n)
                for s in range(ZH):
                    rows_ref[pl.ds(row, n), s * k : (s + 1) * k] = q_refs[j][cc, za * ZH + s]
    out_ref[...] = lax.dot_general(
        rows_ref[...], p_ref[...], (((1,), (1,)), ((), ())), preferred_element_type=f32
    )


def softmax_kernel(part_ref, ids_ref, ds_ref):
    rows, n = part_ref.shape[1:]
    positive = ids_ref[:, 0:1]
    col = lax.broadcasted_iota(jnp.int32, (rows, n), 1)
    base = (
        (((col >> 3) & 1) << 10)
        + (((col >> 6) & 3) << 8)
        + (((col >> 1) & 3) << 3)
        + (((col >> 4) & 3) << 1)
        + (col & 1)
    )
    logits, top = [], None
    for g in range(G):
        a = part_ref[g * Y]
        for y in range(1, Y):
            a = a + part_ref[g * Y + y]
        a = a * logit_scale
        logits.append(a)
        m = jnp.max(a, axis=1, keepdims=True)
        top = m if top is None else jnp.maximum(top, m)
    total = jnp.zeros((rows, 1), f32)
    pos_logit = jnp.zeros((rows, 1), f32)
    scaled, hot = [], []
    for g in range(G):
        ids = base + g * 32
        onehot = ids == positive
        hard = ids == ids_ref[:, 1:2]
        for h in range(2, ids_ref.shape[1]):
            hard = jnp.logical_or(hard, ids == ids_ref[:, h : h + 1])
        hard = jnp.logical_and(hard, jnp.logical_not(onehot))
        e = jnp.where(hard, hard_weight, 1.0) * jnp.exp(logits[g] - top)
        total = total + jnp.sum(e, axis=1, keepdims=True)
        pos_logit = pos_logit + jnp.sum(jnp.where(onehot, logits[g], 0.0), axis=1, keepdims=True)
        scaled.append(e)
        hot.append(jnp.where(onehot, 1.0, 0.0))
    loss = top + jnp.log(total) - pos_logit
    hi = loss.astype(bf16).astype(f32)
    mid = (loss - hi).astype(bf16).astype(f32)
    lo = loss - hi - mid
    lane = lax.broadcasted_iota(jnp.int32, (rows, LANES), 1)
    side = jnp.where(lane == 0, hi, jnp.where(lane == 1, mid, jnp.where(lane == 2, lo, 0.0)))
    side = side.astype(bf16)
    for g in range(G):
        ds = (logit_scale * (scaled[g] / total - hot[g])).astype(bf16)
        for y in range(Y):
            ds_ref[g * Y + y, :, :n] = ds
            ds_ref[g * Y + y, :, n:] = side


def grads_kernel(at_ref, ds_ref, rows_ref, p_ref, *outs):
    qg_refs, (pg_ref, loss_ref) = outs[:X], outs[X:]
    n, k = qg_refs[0].shape[2:]
    np_ = p_ref.shape[0]
    for j in range(X):
        for cc in range(C):
            g = lax.rem(at_ref[0] + j, X) * C + lax.rem(at_ref[1] + cc, C)
            row = pl.multiple_of(g * (ZA * n), ZA * n)
            terms = jnp.dot(
                ds_ref[pl.ds(row, ZA * n), :np_], p_ref[...], preferred_element_type=f32
            ).astype(bf16)
            for za in range(ZA):
                for s in range(ZH):
                    qg_refs[j][cc, za * ZH + s] = terms[za * n : (za + 1) * n, s * k : (s + 1) * k]
            if j == 0 and cc == 0:
                loss_ref[...] = ds_ref[pl.ds(row, ZA * n), np_:]
    pg_ref[...] = lax.dot_general(
        ds_ref[:, :np_], rows_ref[...], (((0,), (0,)), ((), ())), preferred_element_type=f32
    ).astype(bf16)


def on_device(queries, passages, positive, hard_negs):
    nq, k = queries.shape
    own, d = passages.shape
    n = nq // A
    nrow = ZA * n // Y
    width = ZH * k
    za, zh, y = lax.axis_index("za"), lax.axis_index("zh"), lax.axis_index("y")
    at = jnp.stack([lax.axis_index("x"), lax.axis_index("c")]).astype(jnp.int32)

    ids = jnp.concatenate([positive[:, None], hard_negs], axis=1)
    half = lax.rem(y, 2) * nrow
    mine = lax.dynamic_slice_in_dim(ids, (za * ZH + zh) * n + half, nrow, 0)
    other = lax.dynamic_slice_in_dim(ids, ((1 - za) * ZH + zh) * n + half, nrow, 0)
    ids = jnp.where(y // 2 == za, mine, shift(other, "za", 1))

    prow = own * d // k
    send = jnp.concatenate(
        [
            queries.astype(bf16).reshape(A, n, k),
            jnp.broadcast_to(passages.astype(bf16).reshape(1, prow, k), (A, prow, k)),
        ],
        axis=1,
    )
    got = exchange(send, FAR)
    q = got[:, :n]
    theirs, p = lax.optimization_barrier((shift(q, "c", 1), got[:, n:]))
    both = jnp.stack([q, theirs])
    qs = [both] + [shift(both, "x", j) for j in range(1, X)]

    p = p.reshape(A, own, ZH, Y, k).transpose(3, 0, 1, 2, 4).reshape(Y, A * own, width)
    p = jnp.broadcast_to(p[None], (ZB,) + p.shape).reshape(B, A * own, width)
    p = exchange(p, NEAR).reshape(B * A * own, width)
    np_ = p.shape[0]

    parts, rows = pl.pallas_call(
        logits_kernel,
        in_specs=[scalars] + [whole] * (X + 1),
        out_specs=(whole, whole),
        out_shape=(
            jax.ShapeDtypeStruct((G * ZA * n, np_), f32),
            jax.ShapeDtypeStruct((G * ZA * n, width), bf16),
        ),
        compiler_params=params,
        name="logits",
    )(at, *qs, p)
    parts = exchange(parts.reshape(G * Y, nrow, np_), PLANE)

    ds = pl.pallas_call(
        softmax_kernel,
        out_shape=jax.ShapeDtypeStruct((G * Y, nrow, np_ + LANES), bf16),
        compiler_params=params,
        name="softmax",
    )(parts, ids)
    ds = exchange(ds, PLANE).reshape(G * ZA * n, np_ + LANES)

    *qg, pg, loss = pl.pallas_call(
        grads_kernel,
        in_specs=[scalars] + [whole] * 3,
        out_specs=tuple([whole] * (X + 2)),
        out_shape=tuple(
            [jax.ShapeDtypeStruct((C, A, n, k), bf16)] * X
            + [
                jax.ShapeDtypeStruct((np_, width), bf16),
                jax.ShapeDtypeStruct((ZA * n, LANES), bf16),
            ]
        ),
        compiler_params=params,
        name="grads",
    )(at, ds, rows, p)

    terms = [qg[0]] + [shift(qg[j], "x", j) for j in range(1, X)]
    pg = exchange(pg.reshape(B, A * own, width), NEAR)
    terms, pg = lax.optimization_barrier((terms, pg))
    pg = jnp.sum(pg.astype(f32).reshape(ZB, Y, A * own, width), axis=0).astype(bf16)
    pg = pg.reshape(Y, A, own, ZH, k).transpose(1, 2, 3, 0, 4).reshape(A, prow, k)
    pair = sum(t.astype(f32) for t in terms)
    theirs = shift(pair[1].astype(bf16), "c", 1)
    qg = (pair[0] + theirs.astype(f32)).astype(bf16)

    loss = loss.reshape(ZA, n, LANES)[:, :, :3].transpose(0, 2, 1).reshape(ZA, 1, 3 * n)
    loss = jnp.pad(loss, ((0, 0), (0, 7), (0, k - 3 * n)))
    loss = jnp.broadcast_to(loss[:, None], (ZA, ZH, 8, k)).reshape(A, 8, k)
    got = exchange(jnp.concatenate([qg, pg, loss], axis=1), FAR)
    qg = got[:, :n].reshape(nq, k).astype(f32)
    pg = jnp.sum(got[:, n : n + prow].astype(f32), axis=0).reshape(own, d)
    loss = got[:, n + prow, : 3 * n].astype(f32).reshape(A, 3, n)
    row_loss = (loss[:, 0] + loss[:, 1] + loss[:, 2]).reshape(nq)
    return row_loss, qg, pg


def solution(mesh):
    fine = Mesh(mesh.devices.reshape(*SIZES.values()), tuple(SIZES))
    dp, sub = ("za", "zb", "x", "c"), ("zh", "y")
    return jax.shard_map(
        on_device,
        mesh=fine,
        in_specs=(P(dp, sub), P(dp + sub, None), P(dp), P(dp, None)),
        out_specs=(P(dp), P(dp, sub), P(dp + sub, None)),
        check_vma=False,
    )
```

```python
import math

import jax
import jax.numpy as jnp
from jax import lax
from jax.experimental import pallas as pl
from jax.experimental.pallas import tpu as pltpu
from jax.sharding import Mesh, PartitionSpec as P

D = 4096
SIZES = {"za": 2, "zb": 4, "x": 4, "c": 2, "zh": 4, "y": 4}
ZA, ZB, X, C, ZH, Y = SIZES.values()
FAR = ("za", "zh")
NEAR = ("zb", "y")
PLANE = ("x", "c", "y")
G = X * C
A = ZA * ZH
B = ZB * Y
LANES = 128
hard_weight = 4.0
logit_scale = 4.0 / math.sqrt(D)
bf16, f32 = jnp.bfloat16, jnp.float32
params = pltpu.CompilerParams(vmem_limit_bytes=40 * 2**20)
whole = pl.BlockSpec(memory_space=pltpu.VMEM)
scalars = pl.BlockSpec(memory_space=pltpu.SMEM)


def exchange(x, axes):
    return lax.all_to_all(x, axes, 0, 0, tiled=True)


def shift(x, axis, by):
    n = SIZES[axis]
    return lax.ppermute(x, axis, [(i, (i + by) % n) for i in range(n)])


def logits_kernel(at_ref, *refs):
    mine, theirs, (first_ref, p_ref, out_ref, rows_ref) = refs[:X], refs[X], refs[X + 1 :]
    n, k = first_ref.shape[1:]
    for j in range(X):
        for cc in range(C):
            g = lax.rem(at_ref[0] + X - j, X) * C + lax.rem(at_ref[1] + cc, C)
            block = mine[j] if cc == 0 else first_ref if j == 0 else theirs.at[j - 1]
            for za in range(ZA):
                row = pl.multiple_of(g * (ZA * n) + za * n, n)
                for s in range(ZH):
                    rows_ref[pl.ds(row, n), s * k : (s + 1) * k] = block[za * ZH + s]
    out_ref[...] = lax.dot_general(
        rows_ref[...], p_ref[...], (((1,), (1,)), ((), ())), preferred_element_type=f32
    )


def softmax_kernel(part_ref, ids_ref, ds_ref, side_ref):
    rows, n = part_ref.shape[1:]
    positive = ids_ref[:, 0:1]
    col = lax.broadcasted_iota(jnp.int32, (rows, n), 1)
    base = (
        (((col >> 3) & 1) << 10)
        + (((col >> 6) & 3) << 8)
        + (((col >> 1) & 3) << 3)
        + (((col >> 4) & 3) << 1)
        + (col & 1)
    )
    logits, top = [], None
    for g in range(G):
        a = part_ref[g * Y]
        for y in range(1, Y):
            a = a + part_ref[g * Y + y]
        a = a * logit_scale
        logits.append(a)
        m = jnp.max(a, axis=1, keepdims=True)
        top = m if top is None else jnp.maximum(top, m)
    total = jnp.zeros((rows, 1), f32)
    pos_logit = jnp.zeros((rows, 1), f32)
    scaled, hot = [], []
    for g in range(G):
        ids = base + g * 32
        onehot = ids == positive
        hard = ids == ids_ref[:, 1:2]
        for h in range(2, ids_ref.shape[1]):
            hard = jnp.logical_or(hard, ids == ids_ref[:, h : h + 1])
        hard = jnp.logical_and(hard, jnp.logical_not(onehot))
        e = jnp.where(hard, hard_weight, 1.0) * jnp.exp(logits[g] - top)
        total = total + jnp.sum(e, axis=1, keepdims=True)
        pos_logit = pos_logit + jnp.sum(jnp.where(onehot, logits[g], 0.0), axis=1, keepdims=True)
        scaled.append(e)
        hot.append(jnp.where(onehot, 1.0, 0.0))
    loss = top + jnp.log(total) - pos_logit
    hi = loss.astype(bf16).astype(f32)
    mid = (loss - hi).astype(bf16).astype(f32)
    lo = loss - hi - mid
    lane = lax.broadcasted_iota(jnp.int32, (rows, LANES), 1)
    side = jnp.where(lane == 0, hi, jnp.where(lane == 1, mid, jnp.where(lane == 2, lo, 0.0)))
    side_ref[...] = side.astype(bf16)
    for g in range(G):
        ds = (logit_scale * (scaled[g] / total - hot[g])).astype(bf16)
        for y in range(Y):
            ds_ref[g * Y + y] = ds


def grads_kernel(at_ref, ds_ref, side_ref, rows_ref, p_ref, qg_ref, pg_ref):
    n, k = qg_ref.shape[3:]
    width = rows_ref.shape[1]
    for cc in range(C):
        for j in range(X):
            g = lax.rem(at_ref[0] + j, X) * C + lax.rem(at_ref[1] + cc, C)
            row = pl.multiple_of(g * (ZA * n), ZA * n)
            terms = jnp.dot(
                ds_ref[pl.ds(row, ZA * n), :], p_ref[...], preferred_element_type=f32
            ).astype(bf16)
            for za in range(ZA):
                for s in range(ZH):
                    qg_ref[cc, j, za * ZH + s] = terms[za * n : (za + 1) * n, s * k : (s + 1) * k]
    pg_ref[:, :width] = lax.dot_general(
        ds_ref[...], rows_ref[...], (((0,), (0,)), ((), ())), preferred_element_type=f32
    ).astype(bf16)
    nrow = side_ref.shape[0]
    for b in range(pg_ref.shape[0] // nrow):
        pg_ref[b * nrow : (b + 1) * nrow, width:] = side_ref[...]


def on_device(queries, passages, positive, hard_negs):
    nq, k = queries.shape
    own, d = passages.shape
    n = nq // A
    nrow = ZA * n // Y
    width = ZH * k
    za, zh, y = lax.axis_index("za"), lax.axis_index("zh"), lax.axis_index("y")
    at = jnp.stack([lax.axis_index("x"), lax.axis_index("c")]).astype(jnp.int32)

    ids = jnp.concatenate([positive[:, None], hard_negs], axis=1)
    half = lax.rem(y, 2) * nrow
    mine = lax.dynamic_slice_in_dim(ids, (za * ZH + zh) * n + half, nrow, 0)
    other = lax.dynamic_slice_in_dim(ids, ((1 - za) * ZH + zh) * n + half, nrow, 0)
    ids = jnp.where(y // 2 == za, mine, shift(other, "za", 1))

    prow = own * d // k
    send = jnp.concatenate(
        [
            queries.astype(bf16).reshape(A, n, k),
            jnp.broadcast_to(passages.astype(bf16).reshape(1, prow, k), (A, prow, k)),
        ],
        axis=1,
    )
    got = exchange(send, FAR)
    q = got[:, :n]
    qs = [q] + [shift(q, "x", j) for j in range(1, X)]
    first = shift(q, "c", 1)
    theirs = shift(jnp.stack(qs[1:]), "c", 1)

    p = got[:, n:].reshape(A, own, ZH, Y, k).transpose(3, 0, 1, 2, 4).reshape(Y, A * own, width)
    p = jnp.broadcast_to(p[None], (ZB,) + p.shape).reshape(B, A * own, width)
    p = exchange(p, NEAR).reshape(B * A * own, width)
    np_ = p.shape[0]

    parts, rows = pl.pallas_call(
        logits_kernel,
        in_specs=[scalars] + [whole] * (X + 3),
        out_specs=(whole, whole),
        out_shape=(
            jax.ShapeDtypeStruct((G * ZA * n, np_), f32),
            jax.ShapeDtypeStruct((G * ZA * n, width), bf16),
        ),
        compiler_params=params,
        name="logits",
    )(at, *qs, theirs, first, p)
    parts = exchange(parts.reshape(G * Y, nrow, np_), PLANE)

    ds, side = pl.pallas_call(
        softmax_kernel,
        out_shape=(
            jax.ShapeDtypeStruct((G * Y, nrow, np_), bf16),
            jax.ShapeDtypeStruct((nrow, LANES), bf16),
        ),
        compiler_params=params,
        name="softmax",
    )(parts, ids)
    ds = exchange(ds, PLANE).reshape(G * ZA * n, np_)

    qg, pg = pl.pallas_call(
        grads_kernel,
        in_specs=[scalars] + [whole] * 4,
        out_specs=(whole, whole),
        out_shape=(
            jax.ShapeDtypeStruct((C, X, A, n, k), bf16),
            jax.ShapeDtypeStruct((np_, width + LANES), bf16),
        ),
        compiler_params=params,
        name="grads",
    )(at, ds, side, rows, p)

    pg = exchange(pg.reshape(B, A * own, width + LANES), NEAR)
    pair = (qg[0].astype(f32) + shift(qg[1], "c", 1).astype(f32)).astype(bf16)
    terms = [pair[0]] + [shift(pair[j], "x", j) for j in range(1, X)]
    terms, pg = lax.optimization_barrier((terms, pg))
    qg = sum(t.astype(f32) for t in terms).astype(bf16)
    side = lax.dynamic_slice_in_dim(pg, lax.axis_index("zb") * Y, Y, 0)[:, :, width : width + 3]
    pg = pg[:, :, :width].astype(f32).reshape(ZB, Y, A * own, width)
    pg = jnp.sum(pg, axis=0).astype(bf16)
    pg = pg.reshape(Y, A, own, ZH, k).transpose(1, 2, 3, 0, 4).reshape(A, prow, k)

    loss = side.reshape(ZA, n, 3).transpose(0, 2, 1).reshape(ZA, 1, 3 * n)
    loss = jnp.pad(loss, ((0, 0), (0, 7), (0, k - 3 * n)))
    loss = jnp.broadcast_to(loss[:, None], (ZA, ZH, 8, k)).reshape(A, 8, k)
    got = exchange(jnp.concatenate([qg, pg, loss], axis=1), FAR)
    qg = got[:, :n].reshape(nq, k).astype(f32)
    pg = jnp.sum(got[:, n : n + prow].astype(f32), axis=0).reshape(own, d)
    loss = got[:, n + prow, : 3 * n].astype(f32).reshape(A, 3, n)
    row_loss = (loss[:, 0] + loss[:, 1] + loss[:, 2]).reshape(nq)
    return row_loss, qg, pg


def solution(mesh):
    fine = Mesh(mesh.devices.reshape(*SIZES.values()), tuple(SIZES))
    dp, sub = ("za", "zb", "x", "c"), ("zh", "y")
    return jax.shard_map(
        on_device,
        mesh=fine,
        in_specs=(P(dp, sub), P(dp + sub, None), P(dp), P(dp, None)),
        out_specs=(P(dp), P(dp, sub), P(dp + sub, None)),
        check_vma=False,
    )
```

```python
import math

import jax
import jax.numpy as jnp
from jax import lax
from jax.experimental import pallas as pl
from jax.experimental.pallas import tpu as pltpu
from jax.sharding import Mesh, PartitionSpec as P

D = 4096
SIZES = {"za": 2, "zb": 4, "x": 4, "c": 2, "zh": 4, "y": 4}
ZA, ZB, X, C, ZH, Y = SIZES.values()
FAR = ("za", "zh")
A = ZA * ZH
NEAR = ("zb", "y")
PLANE = ("x", "y")
LANES = 128
hard_weight = 4.0
logit_scale = 4.0 / math.sqrt(D)
bf16, f32 = jnp.bfloat16, jnp.float32
params = pltpu.CompilerParams(vmem_limit_bytes=40 * 2**20)
whole = pl.BlockSpec(memory_space=pltpu.VMEM)
scalars = pl.BlockSpec(memory_space=pltpu.SMEM)


def exchange(x, axes):
    return lax.all_to_all(x, axes, 0, 0, tiled=True)


def shift(x, axis, by):
    n = SIZES[axis]
    return lax.ppermute(x, axis, [(i, (i + by) % n) for i in range(n)])


def logits_kernel(at_ref, *refs):
    q_refs, (p_ref, far_ref, out_ref, rows_ref) = refs[:X], refs[X:]
    n, k = q_refs[0].shape[1:]
    np_ = p_ref.shape[0]
    for j in range(X):
        g = lax.rem(at_ref[0] + X - j, X)
        for za in range(ZA):
            row = pl.multiple_of(g * (ZA * n) + za * n, n)
            for s in range(ZH):
                rows_ref[pl.ds(row, n), s * k : (s + 1) * k] = q_refs[j][za * ZH + s]
    for cc, ref in enumerate((p_ref, far_ref)):
        out_ref[:, cc * np_ : (cc + 1) * np_] = lax.dot_general(
            rows_ref[...], ref[...], (((1,), (1,)), ((), ())), preferred_element_type=f32
        )


def softmax_kernel(at_ref, part_ref, ids_ref, ds_ref, side_ref):
    rows, n = part_ref.shape[1:]
    positive = ids_ref[:, 0:1]
    col = lax.broadcasted_iota(jnp.int32, (rows, n), 1)
    base = (
        (((col >> 3) & 1) << 10)
        + (((col >> 6) & 3) << 8)
        + (((col >> 8) & 1) << 5)
        + (((col >> 1) & 3) << 3)
        + (((col >> 4) & 3) << 1)
        + (col & 1)
    ) ^ (at_ref[1] * 32)
    logits, top = [], None
    for g in range(X):
        a = part_ref[g * Y]
        for y in range(1, Y):
            a = a + part_ref[g * Y + y]
        a = a * logit_scale
        logits.append(a)
        m = jnp.max(a, axis=1, keepdims=True)
        top = m if top is None else jnp.maximum(top, m)
    total = jnp.zeros((rows, 1), f32)
    pos_logit = jnp.zeros((rows, 1), f32)
    scaled, hot = [], []
    for g in range(X):
        ids = base + g * 64
        onehot = ids == positive
        hard = ids == ids_ref[:, 1:2]
        for h in range(2, ids_ref.shape[1]):
            hard = jnp.logical_or(hard, ids == ids_ref[:, h : h + 1])
        hard = jnp.logical_and(hard, jnp.logical_not(onehot))
        e = jnp.where(hard, hard_weight, 1.0) * jnp.exp(logits[g] - top)
        total = total + jnp.sum(e, axis=1, keepdims=True)
        pos_logit = pos_logit + jnp.sum(jnp.where(onehot, logits[g], 0.0), axis=1, keepdims=True)
        scaled.append(e)
        hot.append(jnp.where(onehot, 1.0, 0.0))
    loss = top + jnp.log(total) - pos_logit
    hi = loss.astype(bf16).astype(f32)
    mid = (loss - hi).astype(bf16).astype(f32)
    lo = loss - hi - mid
    lane = lax.broadcasted_iota(jnp.int32, (rows, LANES), 1)
    side = jnp.where(lane == 0, hi, jnp.where(lane == 1, mid, jnp.where(lane == 2, lo, 0.0)))
    side_ref[...] = side
    for g in range(X):
        ds = (logit_scale * (scaled[g] / total - hot[g])).astype(bf16)
        for y in range(Y):
            ds_ref[g * Y + y] = ds


def grads_kernel(at_ref, ds_ref, side_ref, rows_ref, p_ref, far_ref, qg_ref, pg_ref, away_ref):
    n, k = qg_ref.shape[2:]
    np_, width = p_ref.shape
    away_ref[...] = lax.dot_general(
        ds_ref[:, np_:], rows_ref[...], (((0,), (0,)), ((), ())), preferred_element_type=f32
    ).astype(bf16)
    pg_ref[:, :width] = lax.dot_general(
        ds_ref[:, :np_], rows_ref[...], (((0,), (0,)), ((), ())), preferred_element_type=f32
    )
    nrow = side_ref.shape[0]
    for b in range(np_ // nrow):
        pg_ref[b * nrow : (b + 1) * nrow, width:] = side_ref[...]
    for j in range(X):
        row = pl.multiple_of(lax.rem(at_ref[0] + j, X) * (ZA * n), ZA * n)
        ds = ds_ref[pl.ds(row, ZA * n), :]
        terms = jnp.dot(ds[:, :np_], p_ref[...], preferred_element_type=f32)
        terms = terms + jnp.dot(ds[:, np_:], far_ref[...], preferred_element_type=f32)
        terms = terms.astype(bf16)
        for za in range(ZA):
            for s in range(ZH):
                qg_ref[j, za * ZH + s] = terms[za * n : (za + 1) * n, s * k : (s + 1) * k]


def on_device(queries, passages, positive, hard_negs):
    nq, k = queries.shape
    own, d = passages.shape
    n = nq // A
    nrow = ZA * n // Y
    width = ZH * k
    za, zh, y = lax.axis_index("za"), lax.axis_index("zh"), lax.axis_index("y")
    at = jnp.stack([lax.axis_index("x"), lax.axis_index("c")]).astype(jnp.int32)

    ids = jnp.concatenate([positive[:, None], hard_negs], axis=1)
    half = lax.rem(y, 2) * nrow
    mine = lax.dynamic_slice_in_dim(ids, (za * ZH + zh) * n + half, nrow, 0)
    other = lax.dynamic_slice_in_dim(ids, ((1 - za) * ZH + zh) * n + half, nrow, 0)
    other = shift(other, "za", 1)

    prow = own * d // k
    send = jnp.concatenate(
        [
            queries.astype(bf16).reshape(A, n, k),
            jnp.broadcast_to(passages.astype(bf16).reshape(1, prow, k), (A, prow, k)),
        ],
        axis=1,
    )
    got, other = lax.optimization_barrier((exchange(send, FAR), other))
    ids = jnp.where(y // 2 == za, mine, other)
    q = got[:, :n]
    qs = [q] + [shift(q, "x", j) for j in range(1, X)]

    few = A * own
    p = got[:, n:].reshape(A, own, ZH, Y, k).transpose(3, 0, 1, 2, 4).reshape(Y, few, width)
    p = jnp.broadcast_to(p[None], (ZB,) + p.shape).reshape(ZB * Y, few, width)
    qs, p = lax.optimization_barrier((qs, exchange(p, NEAR)))
    p = p.reshape(ZB * Y * few, width)
    far = shift(p, "c", 1)
    np_ = C * p.shape[0]

    parts, rows = pl.pallas_call(
        logits_kernel,
        in_specs=[scalars] + [whole] * (X + 2),
        out_specs=(whole, whole),
        out_shape=(
            jax.ShapeDtypeStruct((X * ZA * n, np_), f32),
            jax.ShapeDtypeStruct((X * ZA * n, width), bf16),
        ),
        compiler_params=params,
        name="logits",
    )(at, *qs, p, far)
    parts = exchange(parts.reshape(X * Y, nrow, np_), PLANE)

    ds, side = pl.pallas_call(
        softmax_kernel,
        in_specs=[scalars, whole, whole],
        out_specs=(whole, whole),
        out_shape=(
            jax.ShapeDtypeStruct((X * Y, nrow, np_), bf16),
            jax.ShapeDtypeStruct((nrow, LANES), f32),
        ),
        compiler_params=params,
        name="softmax",
    )(at, parts, ids)
    ds = exchange(ds, PLANE).reshape(X * ZA * n, np_)

    qg, pg, away = pl.pallas_call(
        grads_kernel,
        in_specs=[scalars] + [whole] * 5,
        out_specs=(whole, whole, whole),
        out_shape=(
            jax.ShapeDtypeStruct((X, A, n, k), bf16),
            jax.ShapeDtypeStruct((np_ // C, width + LANES), f32),
            jax.ShapeDtypeStruct((np_ // C, width), bf16),
        ),
        compiler_params=params,
        name="grads",
    )(at, ds, side, rows, p, far)

    away = jnp.pad(shift(away, "c", 1), ((0, 0), (0, LANES)))
    pg = (pg + away.astype(f32)).astype(bf16).reshape(ZB * Y, few, width + LANES)
    pg = exchange(pg, NEAR)
    terms = [qg[0]] + [shift(qg[j], "x", j) for j in range(1, X)]
    terms, pg = lax.optimization_barrier((terms, pg))
    qg = sum(t.astype(f32) for t in terms).astype(bf16)
    side = lax.dynamic_slice_in_dim(pg, lax.axis_index("zb") * Y, Y, 0)[:, :, width : width + 3]
    pg = jnp.sum(pg[:, :, :width].astype(f32).reshape(ZB, Y, few, width), axis=0)
    pg = pg.astype(bf16).reshape(Y, A, own, ZH, k).transpose(1, 2, 3, 0, 4).reshape(A, prow, k)

    loss = side.reshape(ZA, n, 3).transpose(0, 2, 1).reshape(ZA, 1, 3 * n)
    loss = jnp.pad(loss, ((0, 0), (0, 7), (0, k - 3 * n)))
    loss = jnp.broadcast_to(loss[:, None], (ZA, ZH, 8, k)).reshape(A, 8, k)
    got = exchange(jnp.concatenate([qg, pg, loss], axis=1), FAR)
    qg = got[:, :n].reshape(nq, k).astype(f32)
    pg = jnp.sum(got[:, n : n + prow].astype(f32), axis=0).reshape(own, d)
    loss = got[:, n + prow, : 3 * n].astype(f32).reshape(A, 3, n)
    row_loss = (loss[:, 0] + loss[:, 1] + loss[:, 2]).reshape(nq)
    return row_loss, qg, pg


def solution(mesh):
    fine = Mesh(mesh.devices.reshape(*SIZES.values()), tuple(SIZES))
    dp, sub = ("za", "zb", "x", "c"), ("zh", "y")
    return jax.shard_map(
        on_device,
        mesh=fine,
        in_specs=(P(dp, sub), P(dp + sub, None), P(dp), P(dp, None)),
        out_specs=(P(dp), P(dp, sub), P(dp + sub, None)),
        check_vma=False,
    )
```

```python
import math

import jax
import jax.numpy as jnp
from jax import lax
from jax.experimental import pallas as pl
from jax.experimental.pallas import tpu as pltpu
from jax.sharding import Mesh, PartitionSpec as P

D = 4096
SIZES = {"za": 2, "zb": 4, "x": 4, "c": 2, "zh": 4, "y": 4}
ZA, ZB, X, C, ZH, Y = SIZES.values()
FAR = ("za", "zh")
A = ZA * ZH
NEAR = ("zb", "y")
PLANE = ("x", "y")
LANES = 128
hard_weight = 4.0
logit_scale = 4.0 / math.sqrt(D)
bf16, f32 = jnp.bfloat16, jnp.float32
params = pltpu.CompilerParams(vmem_limit_bytes=40 * 2**20)
whole = pl.BlockSpec(memory_space=pltpu.VMEM)
scalars = pl.BlockSpec(memory_space=pltpu.SMEM)


def exchange(x, axes):
    return lax.all_to_all(x, axes, 0, 0, tiled=True)


def shift(x, axis, by):
    n = SIZES[axis]
    return lax.ppermute(x, axis, [(i, (i + by) % n) for i in range(n)])


def pack_kernel(q_ref, p_ref, out_ref, rows_ref):
    groups, _, k = out_ref.shape
    n = q_ref.shape[0] // groups
    own, d = p_ref.shape
    for r in range(own):
        for t in range(d // k):
            i = r * (d // k) + t
            rows_ref[i : i + 1, :] = p_ref[r : r + 1, t * k : (t + 1) * k]
    p = rows_ref[...].astype(bf16)
    for g in range(groups):
        out_ref[g, :n] = q_ref[g * n : (g + 1) * n, :].astype(bf16)
        out_ref[g, n:] = p


def logits_kernel(at_ref, *refs):
    q_refs, (p_ref, out_ref, rows_ref) = refs[:X], refs[X:]
    n, k = q_refs[0].shape[1:]
    for j in range(X):
        g = lax.rem(at_ref[0] + X - j, X)
        for za in range(ZA):
            row = pl.multiple_of(g * (ZA * n) + za * n, n)
            for s in range(ZH):
                rows_ref[pl.ds(row, n), s * k : (s + 1) * k] = q_refs[j][za * ZH + s]
    out_ref[...] = lax.dot_general(
        rows_ref[...], p_ref[...], (((1,), (1,)), ((), ())), preferred_element_type=f32
    )


def more_logits_kernel(rows_ref, far_ref, near_ref, out_ref):
    np_ = far_ref.shape[0]
    out_ref[:, :np_] = near_ref[...]
    out_ref[:, np_:] = lax.dot_general(
        rows_ref[...], far_ref[...], (((1,), (1,)), ((), ())), preferred_element_type=f32
    )


def softmax_kernel(at_ref, part_ref, ids_ref, ds_ref, side_ref):
    rows, n = part_ref.shape[1:]
    positive = ids_ref[:, 0:1]
    col = lax.broadcasted_iota(jnp.int32, (rows, n), 1)
    base = (
        (((col >> 3) & 1) << 10)
        + (((col >> 6) & 3) << 8)
        + (((col >> 8) & 1) << 5)
        + (((col >> 1) & 3) << 3)
        + (((col >> 4) & 3) << 1)
        + (col & 1)
    ) ^ (at_ref[1] * 32)
    logits, top = [], None
    for g in range(X):
        a = part_ref[g * Y]
        for y in range(1, Y):
            a = a + part_ref[g * Y + y]
        a = a * logit_scale
        logits.append(a)
        m = jnp.max(a, axis=1, keepdims=True)
        top = m if top is None else jnp.maximum(top, m)
    total = jnp.zeros((rows, 1), f32)
    pos_logit = jnp.zeros((rows, 1), f32)
    scaled, hot = [], []
    for g in range(X):
        ids = base + g * 64
        onehot = ids == positive
        hard = ids == ids_ref[:, 1:2]
        for h in range(2, ids_ref.shape[1]):
            hard = jnp.logical_or(hard, ids == ids_ref[:, h : h + 1])
        hard = jnp.logical_and(hard, jnp.logical_not(onehot))
        e = jnp.where(hard, hard_weight, 1.0) * jnp.exp(logits[g] - top)
        total = total + jnp.sum(e, axis=1, keepdims=True)
        pos_logit = pos_logit + jnp.sum(jnp.where(onehot, logits[g], 0.0), axis=1, keepdims=True)
        scaled.append(e)
        hot.append(jnp.where(onehot, 1.0, 0.0))
    loss = top + jnp.log(total) - pos_logit
    hi = loss.astype(bf16).astype(f32)
    mid = (loss - hi).astype(bf16).astype(f32)
    lo = loss - hi - mid
    lane = lax.broadcasted_iota(jnp.int32, (rows, LANES), 1)
    side = jnp.where(lane == 0, hi, jnp.where(lane == 1, mid, jnp.where(lane == 2, lo, 0.0)))
    side_ref[...] = side
    for g in range(X):
        ds = (logit_scale * (scaled[g] / total - hot[g])).astype(bf16)
        for y in range(Y):
            ds_ref[g * Y + y] = ds


def away_kernel(ds_ref, rows_ref, away_ref):
    np_ = away_ref.shape[0]
    away_ref[...] = lax.dot_general(
        ds_ref[:, np_:], rows_ref[...], (((0,), (0,)), ((), ())), preferred_element_type=f32
    ).astype(bf16)


def grads_kernel(at_ref, ds_ref, side_ref, rows_ref, p_ref, far_ref, qg_ref, pg_ref):
    n, k = qg_ref.shape[2:]
    np_, width = p_ref.shape
    pg_ref[:, :width] = lax.dot_general(
        ds_ref[:, :np_], rows_ref[...], (((0,), (0,)), ((), ())), preferred_element_type=f32
    )
    nrow = side_ref.shape[0]
    for b in range(np_ // nrow):
        pg_ref[b * nrow : (b + 1) * nrow, width:] = side_ref[...]
    for j in range(X):
        row = pl.multiple_of(lax.rem(at_ref[0] + j, X) * (ZA * n), ZA * n)
        ds = ds_ref[pl.ds(row, ZA * n), :]
        terms = jnp.dot(ds[:, :np_], p_ref[...], preferred_element_type=f32)
        terms = terms + jnp.dot(ds[:, np_:], far_ref[...], preferred_element_type=f32)
        terms = terms.astype(bf16)
        for za in range(ZA):
            for s in range(ZH):
                qg_ref[j, za * ZH + s] = terms[za * n : (za + 1) * n, s * k : (s + 1) * k]


def on_device(queries, passages, positive, hard_negs):
    nq, k = queries.shape
    own, d = passages.shape
    n = nq // A
    nrow = ZA * n // Y
    width = ZH * k
    za, zh, y = lax.axis_index("za"), lax.axis_index("zh"), lax.axis_index("y")
    at = jnp.stack([lax.axis_index("x"), lax.axis_index("c")]).astype(jnp.int32)

    ids = jnp.concatenate([positive[:, None], hard_negs], axis=1)
    half = lax.rem(y, 2) * nrow
    mine = lax.dynamic_slice_in_dim(ids, (za * ZH + zh) * n + half, nrow, 0)
    other = lax.dynamic_slice_in_dim(ids, ((1 - za) * ZH + zh) * n + half, nrow, 0)
    other = shift(other, "za", 1)

    prow = own * d // k
    send = pl.pallas_call(
        pack_kernel,
        out_shape=jax.ShapeDtypeStruct((A, n + prow, k), bf16),
        scratch_shapes=[pltpu.VMEM((prow, k), f32)],
        compiler_params=params,
        name="pack",
    )(queries, passages)
    got = exchange(send, FAR)
    ids = jnp.where(y // 2 == za, mine, other)
    q = got[:, :n]
    qs = [q] + [shift(q, "x", j) for j in range(1, X)]

    few = A * own
    p = got[:, n:].reshape(A, own, ZH, Y, k).transpose(3, 0, 1, 2, 4).reshape(Y, few, width)
    p = jnp.broadcast_to(p[None], (ZB,) + p.shape).reshape(ZB * Y, few, width)
    qs, p = lax.optimization_barrier((qs, exchange(p, NEAR)))
    p = p.reshape(ZB * Y * few, width)
    far = shift(p, "c", 1)
    np_ = C * p.shape[0]

    near, rows = pl.pallas_call(
        logits_kernel,
        in_specs=[scalars] + [whole] * (X + 1),
        out_specs=(whole, whole),
        out_shape=(
            jax.ShapeDtypeStruct((X * ZA * n, np_ // C), f32),
            jax.ShapeDtypeStruct((X * ZA * n, width), bf16),
        ),
        compiler_params=params,
        name="logits",
    )(at, *qs, p)
    parts = pl.pallas_call(
        more_logits_kernel,
        out_shape=jax.ShapeDtypeStruct((X * ZA * n, np_), f32),
        compiler_params=params,
        name="more_logits",
    )(rows, far, near)
    parts = exchange(parts.reshape(X * Y, nrow, np_), PLANE)

    ds, side = pl.pallas_call(
        softmax_kernel,
        in_specs=[scalars, whole, whole],
        out_specs=(whole, whole),
        out_shape=(
            jax.ShapeDtypeStruct((X * Y, nrow, np_), bf16),
            jax.ShapeDtypeStruct((nrow, LANES), f32),
        ),
        compiler_params=params,
        name="softmax",
    )(at, parts, ids)
    ds = exchange(ds, PLANE).reshape(X * ZA * n, np_)

    away = pl.pallas_call(
        away_kernel,
        out_shape=jax.ShapeDtypeStruct((np_ // C, width), bf16),
        compiler_params=params,
        name="away",
    )(ds, rows)
    away = shift(away, "c", 1)
    qg, pg = pl.pallas_call(
        grads_kernel,
        in_specs=[scalars] + [whole] * 5,
        out_specs=(whole, whole),
        out_shape=(
            jax.ShapeDtypeStruct((X, A, n, k), bf16),
            jax.ShapeDtypeStruct((np_ // C, width + LANES), f32),
        ),
        compiler_params=params,
        name="grads",
    )(at, ds, side, rows, p, far)

    away = jnp.pad(away, ((0, 0), (0, LANES)))
    pg = (pg + away.astype(f32)).astype(bf16).reshape(ZB * Y, few, width + LANES)
    pg = exchange(pg, NEAR)
    terms = [qg[0]] + [shift(qg[j], "x", j) for j in range(1, X)]
    terms, pg = lax.optimization_barrier((terms, pg))
    qg = sum(t.astype(f32) for t in terms).astype(bf16)
    side = lax.dynamic_slice_in_dim(pg, lax.axis_index("zb") * Y, Y, 0)[:, :, width : width + 3]
    pg = jnp.sum(pg[:, :, :width].astype(f32).reshape(ZB, Y, few, width), axis=0)
    pg = pg.astype(bf16).reshape(Y, A, own, ZH, k).transpose(1, 2, 3, 0, 4).reshape(A, prow, k)

    loss = side.reshape(ZA, n, 3).transpose(0, 2, 1).reshape(ZA, 1, 3 * n)
    loss = jnp.pad(loss, ((0, 0), (0, 7), (0, k - 3 * n)))
    loss = jnp.broadcast_to(loss[:, None], (ZA, ZH, 8, k)).reshape(A, 8, k)
    got = exchange(jnp.concatenate([qg, pg, loss], axis=1), FAR)
    qg = got[:, :n].reshape(nq, k).astype(f32)
    pg = jnp.sum(got[:, n : n + prow].astype(f32), axis=0).reshape(own, d)
    loss = got[:, n + prow, : 3 * n].astype(f32).reshape(A, 3, n)
    row_loss = (loss[:, 0] + loss[:, 1] + loss[:, 2]).reshape(nq)
    return row_loss, qg, pg


def solution(mesh):
    fine = Mesh(mesh.devices.reshape(*SIZES.values()), tuple(SIZES))
    dp, sub = ("za", "zb", "x", "c"), ("zh", "y")
    return jax.shard_map(
        on_device,
        mesh=fine,
        in_specs=(P(dp, sub), P(dp + sub, None), P(dp), P(dp, None)),
        out_specs=(P(dp), P(dp, sub), P(dp + sub, None)),
        check_vma=False,
    )
```

```python
import math

import jax
import jax.numpy as jnp
from jax import lax
from jax.experimental import pallas as pl
from jax.experimental.pallas import tpu as pltpu
from jax.sharding import Mesh, PartitionSpec as P

D = 4096
SIZES = {"za": 2, "zb": 4, "x": 4, "c": 2, "zh": 4, "y": 4}
ZA, ZB, X, C, ZH, Y = SIZES.values()
FAR = ("za", "zh")
A = ZA * ZH
NEAR = ("zb", "y")
PLANE = ("x", "y")
LANES = 128
hard_weight = 4.0
logit_scale = 4.0 / math.sqrt(D)
bf16, f32 = jnp.bfloat16, jnp.float32
params = pltpu.CompilerParams(vmem_limit_bytes=40 * 2**20)
whole = pl.BlockSpec(memory_space=pltpu.VMEM)
scalars = pl.BlockSpec(memory_space=pltpu.SMEM)


def exchange(x, axes):
    return lax.all_to_all(x, axes, 0, 0, tiled=True)


def shift(x, axis, by):
    n = SIZES[axis]
    return lax.ppermute(x, axis, [(i, (i + by) % n) for i in range(n)])


def pack_kernel(q_in, p_in, out_ref, q_ref, p_ref, rows_ref, sems):
    copies = [
        pltpu.make_async_copy(p_in, p_ref, sems.at[0]),
        pltpu.make_async_copy(q_in, q_ref, sems.at[1]),
    ]
    for copy in copies:
        copy.start()
    for copy in copies:
        copy.wait()
    groups, _, k = out_ref.shape
    n = q_ref.shape[0] // groups
    own, d = p_ref.shape
    for r in range(own):
        for t in range(d // k):
            i = r * (d // k) + t
            rows_ref[i : i + 1, :] = p_ref[r : r + 1, t * k : (t + 1) * k]
    p = rows_ref[...].astype(bf16)
    for g in range(groups):
        out_ref[g, :n] = q_ref[g * n : (g + 1) * n, :].astype(bf16)
        out_ref[g, n:] = p


def logits_kernel(at_ref, *refs):
    q_refs, (p_ref, out_ref, rows_ref) = refs[:X], refs[X:]
    n, k = q_refs[0].shape[1:]
    for j in range(X):
        g = lax.rem(at_ref[0] + X - j, X)
        for za in range(ZA):
            row = pl.multiple_of(g * (ZA * n) + za * n, n)
            for s in range(ZH):
                rows_ref[pl.ds(row, n), s * k : (s + 1) * k] = q_refs[j][za * ZH + s]
    out_ref[...] = lax.dot_general(
        rows_ref[...], p_ref[...], (((1,), (1,)), ((), ())), preferred_element_type=f32
    )


def more_logits_kernel(rows_ref, far_ref, near_ref, out_ref):
    np_ = far_ref.shape[0]
    out_ref[:, :np_] = near_ref[...]
    out_ref[:, np_:] = lax.dot_general(
        rows_ref[...], far_ref[...], (((1,), (1,)), ((), ())), preferred_element_type=f32
    )


def softmax_kernel(at_ref, part_ref, ids_ref, ds_ref, side_ref):
    rows, n = part_ref.shape[1:]
    positive = ids_ref[:, 0:1]
    col = lax.broadcasted_iota(jnp.int32, (rows, n), 1)
    base = (
        (((col >> 3) & 1) << 10)
        + (((col >> 6) & 3) << 8)
        + (((col >> 8) & 1) << 5)
        + (((col >> 1) & 3) << 3)
        + (((col >> 4) & 3) << 1)
        + (col & 1)
    ) ^ (at_ref[1] * 32)
    logits, top = [], None
    for g in range(X):
        a = part_ref[g * Y]
        for y in range(1, Y):
            a = a + part_ref[g * Y + y]
        a = a * logit_scale
        logits.append(a)
        m = jnp.max(a, axis=1, keepdims=True)
        top = m if top is None else jnp.maximum(top, m)
    total = jnp.zeros((rows, 1), f32)
    pos_logit = jnp.zeros((rows, 1), f32)
    scaled, hot = [], []
    for g in range(X):
        ids = base + g * 64
        onehot = ids == positive
        hard = ids == ids_ref[:, 1:2]
        for h in range(2, ids_ref.shape[1]):
            hard = jnp.logical_or(hard, ids == ids_ref[:, h : h + 1])
        hard = jnp.logical_and(hard, jnp.logical_not(onehot))
        e = jnp.where(hard, hard_weight, 1.0) * jnp.exp(logits[g] - top)
        total = total + jnp.sum(e, axis=1, keepdims=True)
        pos_logit = pos_logit + jnp.sum(jnp.where(onehot, logits[g], 0.0), axis=1, keepdims=True)
        scaled.append(e)
        hot.append(jnp.where(onehot, 1.0, 0.0))
    loss = top + jnp.log(total) - pos_logit
    hi = loss.astype(bf16).astype(f32)
    mid = (loss - hi).astype(bf16).astype(f32)
    lo = loss - hi - mid
    lane = lax.broadcasted_iota(jnp.int32, (rows, LANES), 1)
    side = jnp.where(lane == 0, hi, jnp.where(lane == 1, mid, jnp.where(lane == 2, lo, 0.0)))
    side_ref[...] = side
    for g in range(X):
        ds = (logit_scale * (scaled[g] / total - hot[g])).astype(bf16)
        for y in range(Y):
            ds_ref[g * Y + y] = ds


def away_kernel(ds_ref, rows_ref, away_ref):
    np_ = away_ref.shape[0]
    away_ref[...] = lax.dot_general(
        ds_ref[:, np_:], rows_ref[...], (((0,), (0,)), ((), ())), preferred_element_type=f32
    ).astype(bf16)


def grads_kernel(at_ref, ds_ref, side_ref, rows_ref, p_ref, far_ref, qg_ref, pg_ref):
    n, k = qg_ref.shape[2:]
    np_, width = p_ref.shape
    pg_ref[:, :width] = lax.dot_general(
        ds_ref[:, :np_], rows_ref[...], (((0,), (0,)), ((), ())), preferred_element_type=f32
    )
    nrow = side_ref.shape[0]
    for b in range(np_ // nrow):
        pg_ref[b * nrow : (b + 1) * nrow, width:] = side_ref[...]
    for j in range(X):
        row = pl.multiple_of(lax.rem(at_ref[0] + j, X) * (ZA * n), ZA * n)
        ds = ds_ref[pl.ds(row, ZA * n), :]
        terms = jnp.dot(ds[:, :np_], p_ref[...], preferred_element_type=f32)
        terms = terms + jnp.dot(ds[:, np_:], far_ref[...], preferred_element_type=f32)
        terms = terms.astype(bf16)
        for za in range(ZA):
            for s in range(ZH):
                qg_ref[j, za * ZH + s] = terms[za * n : (za + 1) * n, s * k : (s + 1) * k]


def on_device(queries, passages, positive, hard_negs):
    nq, k = queries.shape
    own, d = passages.shape
    n = nq // A
    nrow = ZA * n // Y
    width = ZH * k
    za, zh, y = lax.axis_index("za"), lax.axis_index("zh"), lax.axis_index("y")
    at = jnp.stack([lax.axis_index("x"), lax.axis_index("c")]).astype(jnp.int32)

    ids = jnp.concatenate([positive[:, None], hard_negs], axis=1)
    half = lax.rem(y, 2) * nrow
    mine = lax.dynamic_slice_in_dim(ids, (za * ZH + zh) * n + half, nrow, 0)
    other = lax.dynamic_slice_in_dim(ids, ((1 - za) * ZH + zh) * n + half, nrow, 0)
    other = shift(other, "za", 1)

    prow = own * d // k
    send = pl.pallas_call(
        pack_kernel,
        in_specs=[pl.BlockSpec(memory_space=pl.ANY)] * 2,
        out_shape=jax.ShapeDtypeStruct((A, n + prow, k), bf16),
        scratch_shapes=[
            pltpu.VMEM((nq, k), f32),
            pltpu.VMEM((own, d), f32),
            pltpu.VMEM((prow, k), f32),
            pltpu.SemaphoreType.DMA((2,)),
        ],
        compiler_params=pltpu.CompilerParams(vmem_limit_bytes=60 * 2**20),
        name="pack",
    )(queries, passages)
    got, other = lax.optimization_barrier((exchange(send, FAR), other))
    ids = jnp.where(y // 2 == za, mine, other)
    q = got[:, :n]
    qs = [q] + [shift(q, "x", j) for j in range(1, X)]

    few = A * own
    p = got[:, n:].reshape(A, own, ZH, Y, k).transpose(3, 0, 1, 2, 4).reshape(Y, few, width)
    p = jnp.broadcast_to(p[None], (ZB,) + p.shape).reshape(ZB * Y, few, width)
    qs, p = lax.optimization_barrier((qs, exchange(p, NEAR)))
    p = p.reshape(ZB * Y * few, width)
    far = shift(p, "c", 1)
    np_ = C * p.shape[0]

    near, rows = pl.pallas_call(
        logits_kernel,
        in_specs=[scalars] + [whole] * (X + 1),
        out_specs=(whole, whole),
        out_shape=(
            jax.ShapeDtypeStruct((X * ZA * n, np_ // C), f32),
            jax.ShapeDtypeStruct((X * ZA * n, width), bf16),
        ),
        compiler_params=params,
        name="logits",
    )(at, *qs, p)
    parts = pl.pallas_call(
        more_logits_kernel,
        out_shape=jax.ShapeDtypeStruct((X * ZA * n, np_), f32),
        compiler_params=params,
        name="more_logits",
    )(rows, far, near)
    parts = exchange(parts.reshape(X * Y, nrow, np_), PLANE)

    ds, side = pl.pallas_call(
        softmax_kernel,
        in_specs=[scalars, whole, whole],
        out_specs=(whole, whole),
        out_shape=(
            jax.ShapeDtypeStruct((X * Y, nrow, np_), bf16),
            jax.ShapeDtypeStruct((nrow, LANES), f32),
        ),
        compiler_params=params,
        name="softmax",
    )(at, parts, ids)
    ds = exchange(ds, PLANE).reshape(X * ZA * n, np_)

    away = pl.pallas_call(
        away_kernel,
        out_shape=jax.ShapeDtypeStruct((np_ // C, width), bf16),
        compiler_params=params,
        name="away",
    )(ds, rows)
    away = shift(away, "c", 1)
    qg, pg = pl.pallas_call(
        grads_kernel,
        in_specs=[scalars] + [whole] * 5,
        out_specs=(whole, whole),
        out_shape=(
            jax.ShapeDtypeStruct((X, A, n, k), bf16),
            jax.ShapeDtypeStruct((np_ // C, width + LANES), f32),
        ),
        compiler_params=params,
        name="grads",
    )(at, ds, side, rows, p, far)

    away = jnp.pad(away, ((0, 0), (0, LANES)))
    pg = (pg + away.astype(f32)).astype(bf16).reshape(ZB * Y, few, width + LANES)
    pg = exchange(pg, NEAR)
    terms = [qg[0]] + [shift(qg[j], "x", j) for j in range(1, X)]
    terms, pg = lax.optimization_barrier((terms, pg))
    qg = sum(t.astype(f32) for t in terms).astype(bf16)
    side = lax.dynamic_slice_in_dim(pg, lax.axis_index("zb") * Y, Y, 0)[:, :, width : width + 3]
    pg = jnp.sum(pg[:, :, :width].astype(f32).reshape(ZB, Y, few, width), axis=0)
    pg = pg.astype(bf16).reshape(Y, A, own, ZH, k).transpose(1, 2, 3, 0, 4).reshape(A, prow, k)

    loss = side.reshape(ZA, n, 3).transpose(0, 2, 1).reshape(ZA, 1, 3 * n)
    loss = jnp.pad(loss, ((0, 0), (0, 7), (0, k - 3 * n)))
    loss = jnp.broadcast_to(loss[:, None], (ZA, ZH, 8, k)).reshape(A, 8, k)
    got = exchange(jnp.concatenate([qg, pg, loss], axis=1), FAR)
    qg = got[:, :n].reshape(nq, k).astype(f32)
    pg = jnp.sum(got[:, n : n + prow].astype(f32), axis=0).reshape(own, d)
    loss = got[:, n + prow, : 3 * n].astype(f32).reshape(A, 3, n)
    row_loss = (loss[:, 0] + loss[:, 1] + loss[:, 2]).reshape(nq)
    return row_loss, qg, pg


def solution(mesh):
    fine = Mesh(mesh.devices.reshape(*SIZES.values()), tuple(SIZES))
    dp, sub = ("za", "zb", "x", "c"), ("zh", "y")
    return jax.shard_map(
        on_device,
        mesh=fine,
        in_specs=(P(dp, sub), P(dp + sub, None), P(dp), P(dp, None)),
        out_specs=(P(dp), P(dp, sub), P(dp + sub, None)),
        check_vma=False,
    )
```

```python
import math

import jax
import jax.numpy as jnp
from jax import lax
from jax.experimental import pallas as pl
from jax.experimental.pallas import tpu as pltpu
from jax.sharding import Mesh, PartitionSpec as P

D = 4096
SIZES = {"za": 2, "zb": 4, "x": 4, "c": 2, "zh": 4, "y": 4}
ZA, ZB, X, C, ZH, Y = SIZES.values()
FAR = ("za", "zh")
A = ZA * ZH
NEAR = ("zb", "y")
PLANE = ("x", "y")
LANES = 128
hard_weight = 4.0
logit_scale = 4.0 / math.sqrt(D)
bf16, f32 = jnp.bfloat16, jnp.float32
params = pltpu.CompilerParams(vmem_limit_bytes=40 * 2**20)
whole = pl.BlockSpec(memory_space=pltpu.VMEM)
scalars = pl.BlockSpec(memory_space=pltpu.SMEM)


def exchange(x, axes):
    return lax.all_to_all(x, axes, 0, 0, tiled=True)


def shift(x, axis, by):
    n = SIZES[axis]
    return lax.ppermute(x, axis, [(i, (i + by) % n) for i in range(n)])


def pack_kernel(q_in, p_in, out_ref, q_ref, p_ref, rows_ref, sems):
    copies = [
        pltpu.make_async_copy(p_in, p_ref, sems.at[0]),
        pltpu.make_async_copy(q_in, q_ref, sems.at[1]),
    ]
    for copy in copies:
        copy.start()
    for copy in copies:
        copy.wait()
    groups, _, k = out_ref.shape
    n = q_ref.shape[0] // groups
    own, d = p_ref.shape
    for r in range(own):
        for t in range(d // k):
            i = r * (d // k) + t
            rows_ref[i : i + 1, :] = p_ref[r : r + 1, t * k : (t + 1) * k]
    p = rows_ref[...].astype(bf16)
    for g in range(groups):
        out_ref[g, :n] = q_ref[g * n : (g + 1) * n, :].astype(bf16)
        out_ref[g, n:] = p


def logits_kernel(at_ref, *refs):
    q_refs, (p_ref, out_ref, rows_ref) = refs[:X], refs[X:]
    n, k = q_refs[0].shape[1:]
    for j in range(X):
        g = lax.rem(at_ref[0] + X - j, X)
        for za in range(ZA):
            row = pl.multiple_of(g * (ZA * n) + za * n, n)
            for s in range(ZH):
                rows_ref[pl.ds(row, n), s * k : (s + 1) * k] = q_refs[j][za * ZH + s]
    out_ref[...] = lax.dot_general(
        rows_ref[...], p_ref[...], (((1,), (1,)), ((), ())), preferred_element_type=f32
    )


def more_logits_kernel(rows_ref, far_ref, near_ref, out_ref):
    np_ = far_ref.shape[0]
    out_ref[:, :np_] = near_ref[...]
    out_ref[:, np_:] = lax.dot_general(
        rows_ref[...], far_ref[...], (((1,), (1,)), ((), ())), preferred_element_type=f32
    )


def softmax_kernel(at_ref, part_ref, ids_ref, ds_ref, side_ref):
    rows, n = part_ref.shape[1:]
    positive = ids_ref[:, 0:1]
    col = lax.broadcasted_iota(jnp.int32, (rows, n), 1)
    base = (
        (((col >> 3) & 1) << 10)
        + (((col >> 6) & 3) << 8)
        + (((col >> 8) & 1) << 5)
        + (((col >> 1) & 3) << 3)
        + (((col >> 4) & 3) << 1)
        + (col & 1)
    ) ^ (at_ref[1] * 32)
    logits, top = [], None
    for g in range(X):
        a = part_ref[g * Y]
        for y in range(1, Y):
            a = a + part_ref[g * Y + y]
        a = a * logit_scale
        logits.append(a)
        m = jnp.max(a, axis=1, keepdims=True)
        top = m if top is None else jnp.maximum(top, m)
    total = jnp.zeros((rows, 1), f32)
    pos_logit = jnp.zeros((rows, 1), f32)
    scaled, hot = [], []
    for g in range(X):
        ids = base + g * 64
        onehot = ids == positive
        hard = ids == ids_ref[:, 1:2]
        for h in range(2, ids_ref.shape[1]):
            hard = jnp.logical_or(hard, ids == ids_ref[:, h : h + 1])
        hard = jnp.logical_and(hard, jnp.logical_not(onehot))
        e = jnp.where(hard, hard_weight, 1.0) * jnp.exp(logits[g] - top)
        total = total + jnp.sum(e, axis=1, keepdims=True)
        pos_logit = pos_logit + jnp.sum(jnp.where(onehot, logits[g], 0.0), axis=1, keepdims=True)
        scaled.append(e)
        hot.append(jnp.where(onehot, 1.0, 0.0))
    loss = top + jnp.log(total) - pos_logit
    hi = loss.astype(bf16).astype(f32)
    mid = (loss - hi).astype(bf16).astype(f32)
    lo = loss - hi - mid
    lane = lax.broadcasted_iota(jnp.int32, (rows, LANES), 1)
    side = jnp.where(lane == 0, hi, jnp.where(lane == 1, mid, jnp.where(lane == 2, lo, 0.0)))
    side_ref[...] = side
    for g in range(X):
        ds = (logit_scale * (scaled[g] / total - hot[g])).astype(bf16)
        for y in range(Y):
            ds_ref[g * Y + y] = ds


def away_kernel(ds_ref, rows_ref, away_ref):
    np_ = away_ref.shape[0]
    away_ref[...] = lax.dot_general(
        ds_ref[:, np_:], rows_ref[...], (((0,), (0,)), ((), ())), preferred_element_type=f32
    ).astype(bf16)


def grads_kernel(at_ref, ds_ref, side_ref, rows_ref, p_ref, far_ref, qg_ref, pg_ref):
    n, k = qg_ref.shape[2:]
    np_, width = p_ref.shape
    pg_ref[:, :width] = lax.dot_general(
        ds_ref[:, :np_], rows_ref[...], (((0,), (0,)), ((), ())), preferred_element_type=f32
    )
    nrow = side_ref.shape[0]
    for b in range(np_ // nrow):
        pg_ref[b * nrow : (b + 1) * nrow, width:] = side_ref[...]
    for j in range(X):
        row = pl.multiple_of(lax.rem(at_ref[0] + j, X) * (ZA * n), ZA * n)
        ds = ds_ref[pl.ds(row, ZA * n), :]
        terms = jnp.dot(ds[:, :np_], p_ref[...], preferred_element_type=f32)
        terms = terms + jnp.dot(ds[:, np_:], far_ref[...], preferred_element_type=f32)
        terms = terms.astype(bf16)
        for za in range(ZA):
            for s in range(ZH):
                qg_ref[j, za * ZH + s] = terms[za * n : (za + 1) * n, s * k : (s + 1) * k]


def finish_kernel(got_ref, qg_ref, pg_ref):
    groups, _, k = got_ref.shape
    n = qg_ref.shape[0] // groups
    own, d = pg_ref.shape
    prow = own * d // k
    total = jnp.zeros((prow, k), f32)
    for g in range(groups):
        qg_ref[g * n : (g + 1) * n, :] = got_ref[g, :n].astype(f32)
        total = total + got_ref[g, n : n + prow].astype(f32)
    for i in range(prow):
        r, t = divmod(i, d // k)
        pg_ref[r : r + 1, t * k : (t + 1) * k] = total[i : i + 1, :]


def on_device(queries, passages, positive, hard_negs):
    nq, k = queries.shape
    own, d = passages.shape
    n = nq // A
    nrow = ZA * n // Y
    width = ZH * k
    za, zh, y = lax.axis_index("za"), lax.axis_index("zh"), lax.axis_index("y")
    at = jnp.stack([lax.axis_index("x"), lax.axis_index("c")]).astype(jnp.int32)

    ids = jnp.concatenate([positive[:, None], hard_negs], axis=1)
    half = lax.rem(y, 2) * nrow
    mine = lax.dynamic_slice_in_dim(ids, (za * ZH + zh) * n + half, nrow, 0)
    other = lax.dynamic_slice_in_dim(ids, ((1 - za) * ZH + zh) * n + half, nrow, 0)
    other = shift(other, "za", 1)

    prow = own * d // k
    send = pl.pallas_call(
        pack_kernel,
        in_specs=[pl.BlockSpec(memory_space=pl.ANY)] * 2,
        out_shape=jax.ShapeDtypeStruct((A, n + prow, k), bf16),
        scratch_shapes=[
            pltpu.VMEM((nq, k), f32),
            pltpu.VMEM((own, d), f32),
            pltpu.VMEM((prow, k), f32),
            pltpu.SemaphoreType.DMA((2,)),
        ],
        compiler_params=pltpu.CompilerParams(vmem_limit_bytes=60 * 2**20),
        name="pack",
    )(queries, passages)
    got, other = lax.optimization_barrier((exchange(send, FAR), other))
    ids = jnp.where(y // 2 == za, mine, other)
    q = got[:, :n]
    qs = [q] + [shift(q, "x", j) for j in range(1, X)]

    few = A * own
    p = got[:, n:].reshape(A, own, ZH, Y, k).transpose(3, 0, 1, 2, 4).reshape(Y, few, width)
    p = jnp.broadcast_to(p[None], (ZB,) + p.shape).reshape(ZB * Y, few, width)
    qs, p = lax.optimization_barrier((qs, exchange(p, NEAR)))
    p = p.reshape(ZB * Y * few, width)
    far = shift(p, "c", 1)
    np_ = C * p.shape[0]

    near, rows = pl.pallas_call(
        logits_kernel,
        in_specs=[scalars] + [whole] * (X + 1),
        out_specs=(whole, whole),
        out_shape=(
            jax.ShapeDtypeStruct((X * ZA * n, np_ // C), f32),
            jax.ShapeDtypeStruct((X * ZA * n, width), bf16),
        ),
        compiler_params=params,
        name="logits",
    )(at, *qs, p)
    parts = pl.pallas_call(
        more_logits_kernel,
        out_shape=jax.ShapeDtypeStruct((X * ZA * n, np_), f32),
        compiler_params=params,
        name="more_logits",
    )(rows, far, near)
    parts = exchange(parts.reshape(X * Y, nrow, np_), PLANE)

    ds, side = pl.pallas_call(
        softmax_kernel,
        in_specs=[scalars, whole, whole],
        out_specs=(whole, whole),
        out_shape=(
            jax.ShapeDtypeStruct((X * Y, nrow, np_), bf16),
            jax.ShapeDtypeStruct((nrow, LANES), f32),
        ),
        compiler_params=params,
        name="softmax",
    )(at, parts, ids)
    ds = exchange(ds, PLANE).reshape(X * ZA * n, np_)

    away = pl.pallas_call(
        away_kernel,
        out_shape=jax.ShapeDtypeStruct((np_ // C, width), bf16),
        compiler_params=params,
        name="away",
    )(ds, rows)
    away = shift(away, "c", 1)
    qg, pg = pl.pallas_call(
        grads_kernel,
        in_specs=[scalars] + [whole] * 5,
        out_specs=(whole, whole),
        out_shape=(
            jax.ShapeDtypeStruct((X, A, n, k), bf16),
            jax.ShapeDtypeStruct((np_ // C, width + LANES), f32),
        ),
        compiler_params=params,
        name="grads",
    )(at, ds, side, rows, p, far)

    away = jnp.pad(away, ((0, 0), (0, LANES)))
    pg = (pg + away.astype(f32)).astype(bf16).reshape(ZB * Y, few, width + LANES)
    pg = exchange(pg, NEAR)
    terms = [qg[0]] + [shift(qg[j], "x", j) for j in range(1, X)]
    terms, pg = lax.optimization_barrier((terms, pg))
    qg = sum(t.astype(f32) for t in terms).astype(bf16)
    side = lax.dynamic_slice_in_dim(pg, lax.axis_index("zb") * Y, Y, 0)[:, :, width : width + 3]
    pg = jnp.sum(pg[:, :, :width].astype(f32).reshape(ZB, Y, few, width), axis=0)
    pg = pg.astype(bf16).reshape(Y, A, own, ZH, k).transpose(1, 2, 3, 0, 4).reshape(A, prow, k)

    loss = side.reshape(ZA, n, 3).transpose(0, 2, 1).reshape(ZA, 1, 3 * n)
    loss = jnp.pad(loss, ((0, 0), (0, 7), (0, k - 3 * n)))
    loss = jnp.broadcast_to(loss[:, None], (ZA, ZH, 8, k)).reshape(A, 8, k)
    got = exchange(jnp.concatenate([qg, pg, loss], axis=1), FAR)
    qg, pg = pl.pallas_call(
        finish_kernel,
        out_shape=(
            jax.ShapeDtypeStruct((nq, k), f32),
            jax.ShapeDtypeStruct((own, d), f32),
        ),
        compiler_params=params,
        name="finish",
    )(got)
    loss = got[:, n + prow, : 3 * n].astype(f32).reshape(A, 3, n)
    row_loss = (loss[:, 0] + loss[:, 1] + loss[:, 2]).reshape(nq)
    return row_loss, qg, pg


def solution(mesh):
    fine = Mesh(mesh.devices.reshape(*SIZES.values()), tuple(SIZES))
    dp, sub = ("za", "zb", "x", "c"), ("zh", "y")
    return jax.shard_map(
        on_device,
        mesh=fine,
        in_specs=(P(dp, sub), P(dp + sub, None), P(dp), P(dp, None)),
        out_specs=(P(dp), P(dp, sub), P(dp + sub, None)),
        check_vma=False,
    )
```
